32 devices in a mesh: depth: 16 (over z, y, core), strip: 2 (over x).
Axes of the slice: x: 2, y: 2, z: 4, core: 2. Of those that a mesh axis runs over, the one named last changes fastest.
Arguments:
- sources: bfloat16 [16, 2, 2, 1024, 128], P('depth', 'strip'), may hold values from -6 to 6
- down_state: bfloat16 [16, 2, 2, 1024, 128], P('depth', 'strip'), may hold values from -6 to 6
- up_state: bfloat16 [16, 2, 2, 1024, 128], P('depth', 'strip'), may hold values from -6 to 6
- transfer_op: bfloat16 [16, 2, 2, 1024, 1024], P('depth', 'strip'), may hold values from -0.125 to 0.125
- join_op: bfloat16 [16, 2, 2, 1024, 1024], P('depth', 'strip'), may hold values from -0.125 to 0.125
Outputs:
- down_out: bfloat16 [16, 2, 2, 1024, 128], P('depth', 'strip')
- up_out: bfloat16 [16, 2, 2, 1024, 128], P('depth', 'strip')
The draws below stay inside these ranges and needn't reach their ends.
All inputs are finite; a program needn't handle non-finite values.
Results may differ from the reference program's by a relative error of at most 0.0075.
Values may be sent and summed in bfloat16 or wider, within the bound.
A program may use at most 64 MiB of HBM per device.

```python
import jax
import jax.numpy as jnp
from jax import lax

M = 1024
B = 128
TICKS = 2
PAIRS = 2
LAYERS = 8
N_STRIP = 2


def level_of(own_key, dims, cuts, smallest, largest):
    loudness = 1.0
    for dim, blocks in cuts:
        heights = jax.random.uniform(jax.random.fold_in(jax.random.fold_in(own_key, 6), dim), (blocks,), jnp.float32, smallest / len(cuts), largest / len(cuts))
        loudness = loudness * jnp.repeat(jnp.exp(heights), dims[dim] // blocks).reshape((-1,) + (1,) * (len(dims) - 1 - dim))
    return loudness


def noise(stream_key, extent, width, limit, pieces=(), dtype=jnp.bfloat16):
    values = jax.random.normal(stream_key, extent, jnp.float32) * width
    if len(pieces) > 0:
        values = level_of(stream_key, extent, pieces, -0.22, 0.18) * values
    return jnp.clip(values, min=-limit, max=limit).astype(dtype)


def setup_inputs(seed: int = 0) -> dict:
    splits = jax.random.split(jax.random.key(seed), 6)
    return {
        "sources": noise(splits[0], (LAYERS * PAIRS, N_STRIP, 2, M, B), 0.7, 6.0, ((0, 16), (1, 2))),
        "down_state": noise(splits[1], (LAYERS * PAIRS, N_STRIP, 2, M, B), 1.0, 6.0, ((0, 16), (1, 2))),
        "up_state": noise(splits[2], (LAYERS * PAIRS, N_STRIP, 2, M, B), 1.0, 6.0, ((0, 16), (1, 2))),
        "transfer_op": noise(splits[3], (LAYERS * PAIRS, N_STRIP, 2, M, M), (2 * M) ** -0.5, 0.125, ((0, 16), (1, 2))),
        "join_op": noise(splits[4], (LAYERS * PAIRS, N_STRIP, 2, M, M), (2 * M) ** -0.5, 0.125, ((0, 16), (1, 2))),
    }


def complex_apply(oper, vec, transposed):
    form = "skm,skb->smb" if transposed else "smk,skb->smb"
    op_re = oper[:, 0].astype(jnp.float32)
    op_im = oper[:, 1].astype(jnp.float32)
    vec_re = vec[:, 0].astype(jnp.float32)
    vec_im = vec[:, 1].astype(jnp.float32)
    real_part = jnp.einsum(form, op_re, vec_re) - jnp.einsum(form, op_im, vec_im)
    imag_part = jnp.einsum(form, op_im, vec_re) + jnp.einsum(form, op_re, vec_im)
    return jnp.stack([real_part, imag_part], axis=1)


def layer_update(items):
    source, from_above, from_below, transfer, joiner = items
    a_trace = (source.astype(jnp.float32) + from_above.astype(jnp.float32)).astype(jnp.bfloat16)
    b_trace = (source.astype(jnp.float32) + from_below.astype(jnp.float32)).astype(jnp.bfloat16)
    partner_a = jnp.flip(a_trace, axis=0)
    partner_b = jnp.flip(b_trace, axis=0)
    joined_a = (a_trace.astype(jnp.float32) + complex_apply(joiner, partner_a, False)).astype(jnp.bfloat16)
    joined_b = (b_trace.astype(jnp.float32) + complex_apply(joiner, partner_b, True)).astype(jnp.bfloat16)
    new_down = complex_apply(transfer, joined_a, False).astype(jnp.bfloat16)
    new_up = complex_apply(transfer, joined_b, True).astype(jnp.bfloat16)
    return new_down, new_up


def reference(sources, down_state, up_state, transfer_op, join_op):
    down = down_state
    upward = up_state
    for tick in range(TICKS):
        blank = jnp.zeros_like(down[:PAIRS])
        in_down = jnp.concatenate([blank, down[:-PAIRS]], axis=0)
        in_up = jnp.concatenate([upward[PAIRS:], blank], axis=0)
        down, upward = lax.map(layer_update, (sources, in_down, in_up, transfer_op, join_op))
    return down, upward
```

```python
import jax
import jax.numpy as jnp
from jax import lax
from jax.experimental import pallas as pl
from jax.experimental.pallas import tpu as pltpu
from jax.sharding import PartitionSpec as P

TICKS = 2
PAIRS = 2
AHEAD = 4
UP, DOWN = 0, 1


def turned(re, im):
    return -im, re


def kernel(
    src, down, up, t_hbm, j_hbm, down_out, up_out,
    s_v, s_t, j_v, t_v, yr, own, xr, st, acc_u, acc_d, x_u, x_d,
    y_send, y_recv, x_send, x_recv, load_sem, out_sem,
):
    f32, bf16 = jnp.float32, jnp.bfloat16
    m, b = src.shape[-2], src.shape[-1]
    ch = b
    nch = m // ch
    ahead = min(AHEAD, nch // 2)
    wide = 2 * ch
    phases = 2 * TICKS
    layer = lax.axis_index("depth")
    count = lax.axis_size("depth")
    strip = lax.axis_index("strip")
    partner = strip + 1 - 2 * lax.rem(strip, 2)
    has_above = layer >= PAIRS
    has_below = layer < count - PAIRS

    load_s = pltpu.make_async_copy(src.at[0, 0], s_v, load_sem.at[0])
    load_j = pltpu.make_async_copy(j_hbm.at[0, 0], j_v, load_sem.at[1])
    load_t = pltpu.make_async_copy(t_hbm.at[0, 0], t_v, load_sem.at[2])
    load_s.start()

    barrier = pltpu.get_barrier_semaphore()
    pl.semaphore_signal(
        barrier, inc=1, device_id={"strip": partner}, device_id_type=pl.DeviceIdType.MESH
    )

    @pl.when(has_above)
    def _():
        pl.semaphore_signal(
            barrier, inc=1, device_id={"depth": layer - PAIRS},
            device_id_type=pl.DeviceIdType.MESH,
        )

    @pl.when(has_below)
    def _():
        pl.semaphore_signal(
            barrier, inc=1, device_id={"depth": layer + PAIRS},
            device_id_type=pl.DeviceIdType.MESH,
        )

    pl.semaphore_wait(barrier, 1 + has_above.astype(jnp.int32) + has_below.astype(jnp.int32))

    def y_copy(p, j):
        tick, flow = divmod(p, 2)
        if tick == 0:
            state = (up, down)[flow]
            source = state.at[0, 0, :, pl.ds(j * ch, ch), :]
        else:
            source = st.at[p - 2, j]
        to = layer - PAIRS if flow == UP else layer + PAIRS
        return pltpu.make_async_remote_copy(
            src_ref=source, dst_ref=yr.at[p, j],
            send_sem=y_send.at[p, j], recv_sem=y_recv.at[p, j],
            device_id={"depth": to}, device_id_type=pl.DeviceIdType.MESH,
        )

    def y_start(g):
        p, j = divmod(g, nch)
        if p < phases:
            @pl.when((has_above, has_below)[p % 2])
            def _():
                y_copy(p, j).start()

    def x_copy(p, j):
        return pltpu.make_async_remote_copy(
            src_ref=own.at[p, j], dst_ref=xr.at[p, j],
            send_sem=x_send.at[p, j], recv_sem=x_recv.at[p, j],
            device_id={"strip": partner}, device_id_type=pl.DeviceIdType.MESH,
        )

    for g in range(ahead):
        y_start(g)
    load_j.start()
    load_t.start()

    @pl.when(jnp.logical_not(has_below))
    def _():
        for tick in range(TICKS):
            yr[2 * tick + UP] = jnp.zeros(yr.shape[1:], bf16)

    @pl.when(jnp.logical_not(has_above))
    def _():
        for tick in range(TICKS):
            yr[2 * tick + DOWN] = jnp.zeros(yr.shape[1:], bf16)

    load_s.wait()

    def stage(p, j):
        tick, flow = divmod(p, 2)

        @pl.when((has_below, has_above)[flow])
        def _():
            y_copy(p, j).wait_recv()

        rows = slice(j * ch, (j + 1) * ch)
        for c in range(2):
            arrived = yr[p, j, c].astype(f32)
            if flow == UP:
                if tick == 0:
                    source = s_v[c, rows, :].astype(f32).T
                    s_t[j, c] = source.astype(bf16)
                    arrived = arrived.T
                else:
                    source = s_t[j, c].astype(f32)
            else:
                source = s_v[c, rows, :].astype(f32)
            total = (source + arrived).astype(bf16)
            own[p, j, c] = total
        x_copy(p, j).start()

    def join(p, k):
        flow = p % 2
        x_copy(p, 2 * k).wait_recv()
        x_copy(p, 2 * k + 1).wait_recv()
        axis = 1 if flow == UP else 0
        re = jnp.concatenate([xr[p, 2 * k, 0], xr[p, 2 * k + 1, 0]], axis=axis)
        im = jnp.concatenate([xr[p, 2 * k, 1], xr[p, 2 * k + 1, 1]], axis=axis)
        first = jnp.concatenate([re, im], axis=1 - axis)
        second = jnp.concatenate(turned(re, im), axis=1 - axis)
        inner = slice(k * wide, (k + 1) * wide)
        if flow == UP:
            for i in range(m // wide):
                cols = slice(i * wide, (i + 1) * wide)
                part = jnp.dot(
                    first, j_v[0, inner, cols], preferred_element_type=f32
                ) + jnp.dot(second, j_v[1, inner, cols], preferred_element_type=f32)
                acc_u[:, cols] = part if k == 0 else acc_u[:, cols] + part
        else:
            part = jnp.dot(
                j_v[0, :, inner], first, preferred_element_type=f32
            ) + jnp.dot(j_v[1, :, inner], second, preferred_element_type=f32)
            acc_d[...] = part if k == 0 else acc_d[...] + part

    def rounded(p):
        for j in range(nch):
            near = slice(j * ch, (j + 1) * ch)
            for c in range(2):
                far = slice(c * b, (c + 1) * b)
                trace = own[p, j, c].astype(f32)
                other = slice((1 - c) * b, (2 - c) * b)
                if p % 2 == UP:
                    joined = (acc_u[far, near] + trace).astype(bf16)
                    x_u[0, far, near] = joined
                    x_u[1, other, near] = joined if c == 0 else -joined
                else:
                    joined = (acc_d[near, far] + trace).astype(bf16)
                    x_d[0, near, far] = joined
                    x_d[1, near, other] = joined if c == 0 else -joined

    def out_copy(p, j):
        result = (up_out, down_out)[p % 2]
        return pltpu.make_async_copy(
            st.at[p, j], result.at[0, 0, :, pl.ds(j * ch, ch), :], out_sem.at[p % 2, j]
        )

    def transfer(p, i):
        tick, flow = divmod(p, 2)
        part = slice(i * wide, (i + 1) * wide)
        if flow == UP:
            value = jnp.dot(
                x_u[0], t_v[0, :, part], preferred_element_type=f32
            ) + jnp.dot(x_u[1], t_v[1, :, part], preferred_element_type=f32)
        else:
            value = jnp.dot(
                t_v[0, part, :], x_d[0], preferred_element_type=f32
            ) + jnp.dot(t_v[1, part, :], x_d[1], preferred_element_type=f32)
        for h in range(2):
            near = slice(h * ch, (h + 1) * ch)
            for c in range(2):
                far = slice(c * b, (c + 1) * b)
                if flow == UP:
                    piece = value[far, near]
                    if tick == TICKS - 1:
                        piece = piece.T
                else:
                    piece = value[near, far]
                st[p, 2 * i + h, c] = piece.astype(bf16)
            if tick == TICKS - 1:
                out_copy(p, 2 * i + h).start()

    pairs = nch // 2
    lag = 2
    todo = {}

    def at(step, call, *args):
        todo.setdefault(step, []).append((call, args))

    end = phases * nch
    for p in range(phases):
        base = p * nch
        for k in range(pairs):
            at(min(base + 2 * k + 1 + lag, end), join, p, k)
        at(min(base + nch + lag, end), rounded, p)
        for i in range(pairs):
            step = base + 2 * nch - ahead + (i if p == phases - 2 else 2 * i)
            at(min(step, end), transfer, p, i)

    for g in range(end):
        p, j = divmod(g, nch)
        stage(p, j)
        if g == 3:
            load_j.wait()
        if g == nch:
            load_t.wait()
        for call, args in todo.get(g, ()):
            call(*args)
        y_start(g + ahead)
    for call, args in todo.get(end, ()):
        call(*args)

    for p in range(phases):
        for j in range(nch):
            x_copy(p, j).wait_send()

            @pl.when((has_above, has_below)[p % 2])
            def _():
                y_copy(p, j).wait_send()
    for p in (phases - 2, phases - 1):
        for j in range(nch):
            out_copy(p, j).wait()


def per_device(sources, down_state, up_state, transfer_op, join_op):
    m, b = sources.shape[-2:]
    nch = m // b
    phases = 2 * TICKS
    bf16, f32 = jnp.bfloat16, jnp.float32
    out = jax.ShapeDtypeStruct(sources.shape, bf16)
    chunked = (phases, nch, 2, b, b)
    return pl.pallas_call(
        kernel,
        out_shape=(out, out),
        in_specs=[pl.BlockSpec(memory_space=pl.ANY)] * 5,
        out_specs=[pl.BlockSpec(memory_space=pl.ANY)] * 2,
        scratch_shapes=[
            pltpu.VMEM((2, m, b), bf16),
            pltpu.VMEM((nch, 2, b, b), bf16),
            pltpu.VMEM((2, m, m), bf16),
            pltpu.VMEM((2, m, m), bf16),
            pltpu.VMEM(chunked, bf16),
            pltpu.VMEM(chunked, bf16),
            pltpu.VMEM(chunked, bf16),
            pltpu.VMEM(chunked, bf16),
            pltpu.VMEM((2 * b, m), f32),
            pltpu.VMEM((m, 2 * b), f32),
            pltpu.VMEM((2, 2 * b, m), bf16),
            pltpu.VMEM((2, m, 2 * b), bf16),
            pltpu.SemaphoreType.DMA((phases, nch)),
            pltpu.SemaphoreType.DMA((phases, nch)),
            pltpu.SemaphoreType.DMA((phases, nch)),
            pltpu.SemaphoreType.DMA((phases, nch)),
            pltpu.SemaphoreType.DMA((3,)),
            pltpu.SemaphoreType.DMA((2, nch)),
        ],
        compiler_params=pltpu.CompilerParams(
            collective_id=0, has_side_effects=True, vmem_limit_bytes=60 * 1024 * 1024
        ),
        cost_estimate=pl.CostEstimate(
            flops=TICKS * 32 * m * m * b, bytes_accessed=8 * m * (m + 2 * b), transcendentals=0
        ),
    )(sources, down_state, up_state, transfer_op, join_op)


def solution(mesh):
    spec = P("depth", "strip", None, None, None)
    return jax.shard_map(
        per_device,
        mesh=mesh,
        in_specs=(spec,) * 5,
        out_specs=(spec, spec),
        check_vma=False,
    )
```
